32 devices in a mesh: parts: 2 (over y), dp: 8 (over z, x), fac: 2 (over core).
Axes of the slice: x: 2, y: 2, z: 4, core: 2. Of those that a mesh axis runs over, the one named last changes fastest.
Arguments:
- acts: bfloat16 [2816, 14336], P(('parts', 'dp'), 'fac'), parts along dimension 0, may hold values from -6 to 6
- grads: bfloat16 [2816, 4096], P(('parts', 'dp'), 'fac'), parts along dimension 0, may hold values from -6 to 6
- lengths: int32 [16, 4], P(('parts', 'dp')), parts along dimension 0, may hold values from 1 to 88, 176 in all within a row
- basis_a: bfloat16 [2, 7168, 14336], P('fac', 'dp'), may hold values from -0.046875 to 0.046875
- basis_g: bfloat16 [2, 2048, 4096], P('fac', 'dp'), may hold values from -0.09375 to 0.09375
- coef_a: bfloat16 [14336, 256], P(('dp', 'fac')), may hold values from -0.009765625 to 0.009765625
- coef_g: bfloat16 [4096, 256], P(('dp', 'fac')), may hold values from -0.01953125 to 0.01953125
- eig_a: float32 [14336], P(('dp', 'fac')), may hold values from 0.02 to 2
- eig_g: float32 [4096], P(('dp', 'fac')), may hold values from 0.02 to 2
Outputs:
- scores: float32 [64, 8], P(('parts', 'dp'), 'fac'), parts along dimension 0
The draws below stay inside these ranges and needn't reach their ends.
There are 2 independent parts, one for each index of `parts`. The reference program is written for one: setup_inputs(seed, part) draws one part's arguments, and reference() takes and returns one part's arrays. A program takes and returns all parts, laid end to end along the dimension named above; an argument that names none is the same for every part. Nothing has to cross between parts.
Inputs may be any that keep to these rules, and one draw needn't show every extreme that they name: `lengths`: in each index of dp the counts sum to 176, and the largest of them is exactly 88.
All inputs are finite; a program needn't handle non-finite values.
Results may differ from the reference program's by a relative error of at most 0.0057.
Values may be sent and summed in bfloat16 or wider, within the bound.
A program may use at most 128 MiB of HBM per device.

```python
import math
import jax
import jax.numpy as jnp
import numpy as np
from jax import lax

DM = 4096
FF = 14336
RANK = 32
QN = 8
TOK_DEV = 176
DOCS = 4
SEQMAX = 88
QR = 256
TOKENS = 1408
N_DP = 8
N_FAC = 2


def block_scale(own_key, dims, split, smallest, largest):
    gain = 1.0
    for axis_at, parts in split:
        draws = jax.random.uniform(jax.random.fold_in(jax.random.fold_in(own_key, 6), axis_at), (parts,), jnp.float32, smallest / len(split), largest / len(split))
        gain = gain * jnp.repeat(jnp.exp(draws), dims[axis_at] // parts).reshape((-1,) + (1,) * (len(dims) - 1 - axis_at))
    return gain


def length_profile(amount, total, limit, skew):
    portions = [(1 << 20) // math.isqrt(rank ** skew) + 1 for rank in range(2, amount + 1)]
    spare, holding = total - limit - (amount - 1), [1] * (amount - 1)
    while spare > 0:
        movable = [i for i in range(amount - 1) if holding[i] < limit]
        mass, left = sum([portions[i] for i in movable]), spare
        for i in movable:
            more = min(limit - holding[i], max(1, left * portions[i] // mass), spare)
            holding[i] = holding[i] + more
            spare = spare - more
    return np.array([limit] + holding)


def uneven_parts(rng, amount, total, reach, lean):
    if amount == 2:
        one = jax.random.randint(rng, (), max(1, total - reach), min(reach, total - 1) + 1)
        return jnp.stack([one, total - one])
    tallies = jnp.asarray(length_profile(amount, total, reach, lean), jnp.int32)
    pairs = (amount - 1) // 2
    giver, receiver = tallies[1:1 + 2 * pairs:2], tallies[2:2 + 2 * pairs:2]
    room = jnp.minimum(giver - 1, reach - receiver)
    shifted = jax.random.randint(jax.random.fold_in(rng, 1), (pairs,), 0, 1 << 20) % (room + 1)
    tallies = tallies.at[1:1 + 2 * pairs:2].set(giver - shifted).at[2:2 + 2 * pairs:2].set(receiver + shifted)
    return tallies[jax.random.permutation(jax.random.fold_in(rng, 2), amount)]


def normal_values(stream_key, shape, deviation, reach, cuts=(), held_as=jnp.bfloat16):
    factor_of = block_scale(stream_key, shape, cuts, -0.22, 0.18) if cuts else 1.0
    drawn = jax.random.normal(stream_key, shape, jnp.float32) * deviation * factor_of
    return jnp.minimum(jnp.maximum(drawn, -reach), reach).astype(held_as)


def setup_inputs(seed: int = 0, part: int = 0) -> dict:
    key_list = jax.random.split(jax.random.key(seed), 10)
    part_keys = jax.random.split(jax.random.fold_in(key_list[9], part), 10)
    return {
        "acts": normal_values(part_keys[0], (TOKENS, FF), 1.0, 6.0, ((0, 8), (1, 2))),
        "grads": normal_values(part_keys[1], (TOKENS, DM), 1.0, 6.0, ((0, 8), (1, 2))),
        "lengths": jax.vmap(lambda own: uneven_parts(own, DOCS, TOK_DEV, SEQMAX, 1))(jax.random.split(part_keys[2], N_DP)).reshape((N_DP, DOCS)).astype(jnp.int32),
        "basis_a": normal_values(key_list[3], (N_FAC, FF // N_FAC, FF), FF ** -0.5, 0.046875, ((0, 2), (1, 8))),
        "basis_g": normal_values(key_list[4], (N_FAC, DM // N_FAC, DM), DM ** -0.5, 0.09375, ((0, 2), (1, 8))),
        "coef_a": normal_values(key_list[5], (FF, QR), (25 * FF) ** -0.5, 0.009765625, ((0, 16),)),
        "coef_g": normal_values(key_list[6], (DM, QR), (25 * DM) ** -0.5, 0.01953125, ((0, 16),)),
        "eig_a": jnp.clip(jnp.exp(math.log(2.0) - 4.6051702 * jax.random.uniform(key_list[7], (FF,), jnp.float32) ** block_scale(key_list[7], (FF,), ((0, 16),), -0.2, 0.2)), 0.02, 2.0),
        "eig_g": jnp.clip(jnp.exp(math.log(2.0) - 4.6051702 * jax.random.uniform(key_list[8], (DM,), jnp.float32) ** block_scale(key_list[8], (DM,), ((0, 16),), -0.2, 0.2)), 0.02, 2.0),
    }


damping = 0.1

def reference(acts, grads, lengths, basis_a, basis_g, coef_a, coef_g, eig_a, eig_g):
    scaled_a = (coef_a.astype(jnp.float32) / (eig_a[:, None] + damping)).astype(jnp.bfloat16)
    scaled_g = (coef_g.astype(jnp.float32) / (eig_g[:, None] + damping)).astype(jnp.bfloat16)
    factor_a = jnp.dot(basis_a.reshape(FF, FF), scaled_a, preferred_element_type=jnp.float32).astype(jnp.bfloat16)
    factor_g = jnp.dot(basis_g.reshape(DM, DM), scaled_g, preferred_element_type=jnp.float32).astype(jnp.bfloat16)
    proj_a = jnp.dot(acts, factor_a, preferred_element_type=jnp.float32)
    proj_g = jnp.dot(grads, factor_g, preferred_element_type=jnp.float32)
    products = (proj_a * proj_g).reshape(N_DP, TOK_DEV, QN, RANK).sum(axis=3)
    doc_ends = jnp.cumsum(lengths, axis=1).astype(jnp.int32)
    doc_starts = (doc_ends - lengths).astype(jnp.int32)
    position = jnp.arange(TOK_DEV, dtype=jnp.int32)
    member = ((position[None, :, None] >= doc_starts[:, None, :]) & (position[None, :, None] < doc_ends[:, None, :])).astype(jnp.float32)
    sums = jnp.einsum('ntd,ntq->ndq', member, products, precision=lax.Precision.HIGHEST)
    divisor = jnp.sqrt(RANK * lengths.astype(jnp.float32))
    return (sums / divisor[:, :, None]).reshape(N_DP * DOCS, QN)
```

```python
import functools

import jax
import jax.numpy as jnp
from jax import lax
from jax.experimental import pallas as pl
from jax.experimental.pallas import tpu as pltpu
from jax.sharding import PartitionSpec as P

RANK = 32
LANES = 128


damping = 0.1


def scaled(coef, eig):
    return (coef.astype(jnp.float32) / (eig[:, None] + damping)).astype(jnp.bfloat16)


def on_device(acts, grads, lengths, basis_a, basis_g, coef_a, coef_g, eig_a, eig_g):
    scaled_a = scaled(coef_a, eig_a)
    scaled_g = scaled(coef_g, eig_g)
    part_a = lax.all_gather(scaled_a, ("dp", "fac"), axis=0, tiled=True)
    part_g = lax.all_gather(scaled_g, ("dp", "fac"), axis=0, tiled=True)
    factor_a = jnp.dot(basis_a[0], part_a, preferred_element_type=jnp.float32).astype(jnp.bfloat16)
    factor_g = jnp.dot(basis_g[0], part_g, preferred_element_type=jnp.float32).astype(jnp.bfloat16)
    proj_a = jnp.dot(
        acts,
        lax.all_gather(factor_a, "dp", axis=0, tiled=True),
        preferred_element_type=jnp.float32,
    )
    proj_g = jnp.dot(
        grads,
        lax.all_gather(factor_g, "dp", axis=0, tiled=True),
        preferred_element_type=jnp.float32,
    )
    share_a = lax.psum_scatter(proj_a, "fac", scatter_dimension=1, tiled=True)
    share_g = lax.psum_scatter(proj_g, "fac", scatter_dimension=1, tiled=True)
    tok_rows = acts.shape[0]
    owned_queries = share_a.shape[1] // RANK
    products = (share_a * share_g).reshape(tok_rows, owned_queries, RANK).sum(axis=2)
    counts = lengths[0]
    docs = counts.shape[0]
    before = jnp.arange(docs)[:, None] <= jnp.arange(docs)[None, :]
    doc_ends = jnp.sum(jnp.where(before, counts[:, None], 0), axis=0)
    doc_starts = doc_ends - counts
    position = jnp.arange(tok_rows, dtype=jnp.int32)
    member = (
        (position[:, None] >= doc_starts[None, :]) & (position[:, None] < doc_ends[None, :])
    ).astype(jnp.float32)
    sums = jnp.einsum("td,tq->dq", member, products, precision=lax.Precision.HIGHEST)
    divisor = jnp.sqrt(RANK * counts.astype(jnp.float32))
    return sums / divisor[:, None]


def kernel(
    dims, len_ref, stack, acts, grads, basis_a, basis_g, out,
    coefs, panel_a, panel_g, sum_a, sum_g, give, facs, padded, toks_a, toks_g,
    proj, from_sib, to_y, from_y,
    pa_sem, pg_sem, own_sem,
    line1_s, line1_r, x1_s, x1_r, sib_s, sib_r,
    line2_s, line2_r, x2_s, x2_r, y_s, y_r,
    ta_l, ta_s, ta_r, tg_l, tg_s, tg_r, end_s, end_r,
):
    nz, nx, rows_a, rows_g, docs = dims
    p, d, f = lax.axis_index("parts"), lax.axis_index("dp"), lax.axis_index("fac")
    z, x = d // nx, d % nx
    nd = nz * nx
    half_a, half_g = rows_a // 2, rows_g // 2
    wide = toks_a.shape[3]
    tok_rows = acts.shape[0]

    def dev(pp=None, zz=None, xx=None, ff=None):
        zz = z if zz is None else zz
        xx = x if xx is None else xx
        return (p if pp is None else pp, zz * nx + xx, f if ff is None else ff)

    def send(src, dst, s, r, where):
        return pltpu.make_async_remote_copy(
            src_ref=src, dst_ref=dst, send_sem=s, recv_sem=r,
            device_id=where, device_id_type=pl.DeviceIdType.MESH,
        )

    deep = nx * 2 * rows_a

    def load_panel(zb):
        return pltpu.make_async_copy(
            basis_a.at[0, :, pl.ds(pl.multiple_of(zb * deep, LANES), deep)],
            panel_a.at[zb], pa_sem.at[zb],
        )

    load_g = pltpu.make_async_copy(basis_g.at[0], panel_g, pg_sem)
    own = pltpu.make_async_copy(
        stack.at[:, pl.ds(pl.multiple_of(p * LANES, LANES), LANES)], coefs.at[z, x, f], own_sem
    )
    own.start()
    load_g.start()
    for s in range(nz):
        load_panel(lax.rem(z + s, nz)).start()

    barrier = pltpu.get_barrier_semaphore()
    for where in (dev(pp=1 - p), dev(pp=1 - p, ff=1 - f), dev(ff=1 - f), dev(xx=1 - x)):
        pl.semaphore_signal(barrier, inc=1, device_id=where, device_id_type=pl.DeviceIdType.MESH)

    @pl.when(z > 0)
    def _():
        pl.semaphore_signal(
            barrier, inc=1, device_id=dev(zz=z - 1), device_id_type=pl.DeviceIdType.MESH
        )

    @pl.when(z < nz - 1)
    def _():
        pl.semaphore_signal(
            barrier, inc=1, device_id=dev(zz=z + 1), device_id_type=pl.DeviceIdType.MESH
        )

    pl.semaphore_wait(barrier, 4 + jnp.where(z > 0, 1, 0) + jnp.where(z < nz - 1, 1, 0))
    own.wait()

    def line(block, ss, rr, up, step):
        zb = z - (step - 1) if up else z + (step - 1)
        k = 0 if up else 1
        return send(block(zb, x), block(zb, x), ss.at[k, step], rr.at[k, step],
                    dev(zz=z + 1 if up else z - 1))

    def landed(block, ss, rr, up, step):
        zb = z - step if up else z + step
        k = 0 if up else 1
        return send(block(zb, x), block(zb, x), ss.at[k, step], rr.at[k, step],
                    dev(zz=z - 1 if up else z + 1))

    def across(block, ss, rr, zb, xb):
        return send(block(zb, xb), block(zb, xb), ss.at[zb], rr.at[zb], dev(xx=1 - x))

    def twin(zb, xb, ff):
        return send(coefs.at[zb, xb, ff], coefs.at[zb, xb, ff],
                    sib_s.at[zb, xb], sib_r.at[zb, xb], dev(ff=1 - f))

    def gather(block, ls, lr, xs, xr, extra, use):
        def pass_on(zb):
            across(block, xs, xr, zb, x).start()
            extra(zb, x)

        @pl.when(z < nz - 1)
        def _():
            line(block, ls, lr, True, 1).start()

        @pl.when(z > 0)
        def _():
            line(block, ls, lr, False, 1).start()

        pass_on(z)

        def step(s, carry):
            @pl.when((s < nz) & (z - s >= 0))
            def _():
                landed(block, ls, lr, True, s).wait_recv()

                @pl.when(z < nz - 1)
                def _():
                    line(block, ls, lr, True, s + 1).start()

                pass_on(z - s)

            @pl.when((s < nz) & (z + s < nz))
            def _():
                landed(block, ls, lr, False, s).wait_recv()

                @pl.when(z > 0)
                def _():
                    line(block, ls, lr, False, s + 1).start()

                pass_on(z + s)

            def side(j, c):
                zb = z + (s - 1) * (2 * j - 1)

                @pl.when((zb >= 0) & (zb < nz) & ((s > 1) | (j == 0)))
                def _():
                    across(block, xs, xr, zb, 1 - x).wait_recv()
                    extra(zb, 1 - x)
                    use(zb)

                return c

            return lax.fori_loop(0, 2, side, carry)

        lax.fori_loop(1, nz + 1, step, 0)

    def gather_sent(block, ls, lr, xs, xr):
        def step(s, carry):
            @pl.when((z < nz - 1) & (z - s + 1 >= 0))
            def _():
                line(block, ls, lr, True, s).wait_send()

            @pl.when((z > 0) & (z + s - 1 < nz))
            def _():
                line(block, ls, lr, False, s).wait_send()

            return carry

        lax.fori_loop(1, nz, step, 0)

        def crossing(zb, carry):
            across(block, xs, xr, zb, x).wait_send()
            return carry

        lax.fori_loop(0, nz, crossing, 0)

    step_a = rows_a - wide

    def cols_a(db, q):
        return pl.ds(pl.multiple_of(db * rows_a + q * step_a, LANES), wide)

    def cols_g(db, q):
        return pl.ds(pl.multiple_of(db * rows_g + q * half_g, LANES), half_g)

    def own_a(db):
        return pltpu.make_async_copy(acts.at[:, cols_a(db, p)], toks_a.at[p, db], ta_l.at[db])

    def own_g(db):
        return pltpu.make_async_copy(grads.at[:, cols_g(db, p)], toks_g.at[p, db], tg_l.at[db])

    def swap_a(db, q):
        return send(acts.at[:, cols_a(db, 1 - p)], toks_a.at[q, db], ta_s.at[db], ta_r.at[db],
                    dev(pp=1 - p))

    def swap_g(db, q):
        return send(grads.at[:, cols_g(db, 1 - p)], toks_g.at[q, db], tg_s.at[db], tg_r.at[db],
                    dev(pp=1 - p))

    early = (nd + 1) // 2

    def start_swaps(lo, hi):
        def body(db, carry):
            swap_a(db, p).start()
            swap_g(db, p).start()
            return carry

        lax.fori_loop(lo, hi, body, 0)

    def block1(zb, xb):
        return coefs.at[zb, xb, f]

    def extra1(zb, xb):
        twin(zb, xb, f).start()

    sum_a[...] = jnp.zeros_like(sum_a)
    sum_g[...] = jnp.zeros_like(sum_g)
    padded[...] = jnp.zeros_like(padded)
    proj[...] = jnp.zeros_like(proj)

    def use1(zb):
        load_panel(zb).wait()

        @pl.when(zb == z)
        def _():
            load_g.wait()

        for xb in range(nx):
            twin(zb, xb, 1 - f).wait_recv()
        total_a, total_g = sum_a[...], sum_g[...]
        for i in range(nx * 2):
            block = coefs.at[zb, i // 2, i % 2]
            total_a += jnp.dot(
                panel_a[zb, :, i * rows_a:(i + 1) * rows_a], block[:rows_a],
                preferred_element_type=jnp.float32,
            )
            at = pl.multiple_of((zb * nx * 2 + i) * rows_g, LANES)
            total_g += jnp.dot(
                panel_g[:, pl.ds(at, rows_g)], block[rows_a:],
                preferred_element_type=jnp.float32,
            )
        sum_a[...] = total_a
        sum_g[...] = total_g

    start_swaps(0, early)

    def start_own(db, carry):
        own_a(db).start()
        own_g(db).start()
        return carry

    lax.fori_loop(0, nd, start_own, 0)
    gather(block1, line1_s, line1_r, x1_s, x1_r, extra1, use1)

    def halves(q):
        return (
            sum_a[pl.ds(pl.multiple_of(q * half_a, 16), half_a), :].astype(jnp.bfloat16),
            sum_g[pl.ds(pl.multiple_of(q * half_g, 16), half_g), :].astype(jnp.bfloat16),
        )

    give_a, give_g = halves(1 - p)
    give[:half_a] = give_a
    give[half_a:] = give_g
    send(give, facs.at[z, x, p], y_s, y_r, dev(pp=1 - p)).start()
    keep_a, keep_g = halves(p)
    facs[z, x, p, :half_a] = keep_a
    facs[z, x, p, half_a:] = keep_g
    start_swaps(early, nd)
    send(give, facs.at[z, x, 1 - p], y_s, y_r, dev(pp=1 - p)).wait()

    def block2(zb, xb):
        return facs.at[zb, xb]

    lead = half_a - step_a

    def use2(zb):
        for xb in range(nx):
            db = zb * nx + xb
            own_a(db).wait()
            own_g(db).wait()
            swap_a(db, 1 - p).wait_recv()
            swap_g(db, 1 - p).wait_recv()
            rows = pl.ds(pl.multiple_of(p * lead, 16), half_a)
            for c in range(2):
                padded[rows, c * LANES:(c + 1) * LANES] = facs[zb, xb, c, :half_a]
            fac_g = jnp.concatenate([facs[zb, xb, c, half_a:] for c in range(2)], axis=1)
            fac_a = padded[...]
            for q in range(2):
                proj[0, q] += jnp.dot(toks_a[q, db], fac_a, preferred_element_type=jnp.float32)
                proj[1, q] += jnp.dot(toks_g[q, db], fac_g, preferred_element_type=jnp.float32)

    gather(block2, line2_s, line2_r, x2_s, x2_r, lambda zb, xb: None, use2)

    def half(q):
        return pl.ds(pl.multiple_of(q * LANES, LANES), LANES)

    for ff in range(2):
        to_y[ff] = proj[:, 1 - p, :, ff * LANES:(ff + 1) * LANES].astype(jnp.bfloat16)
    ends = [
        send(to_y.at[f], from_y.at[f], end_s.at[0], end_r.at[0], dev(pp=1 - p)),
        send(to_y.at[1 - f], from_y.at[f], end_s.at[1], end_r.at[1], dev(pp=1 - p, ff=1 - f)),
        send(proj.at[:, p, :, half(1 - f)], from_sib, end_s.at[2], end_r.at[2], dev(ff=1 - f)),
    ]
    for copy in ends:
        copy.start()

    counts = [len_ref[0, i] for i in range(docs)]
    row = lax.broadcasted_iota(jnp.int32, (8, tok_rows), 0)
    position = lax.broadcasted_iota(jnp.int32, (8, tok_rows), 1)
    doc = lax.broadcasted_iota(jnp.int32, (8, LANES), 0)
    member = jnp.zeros((8, tok_rows), jnp.float32)
    size = jnp.ones((8, LANES), jnp.float32)
    begin = jnp.int32(0)
    for i in range(docs):
        stop = begin + counts[i]
        inside = (row == i) & (position >= begin) & (position < stop)
        member = jnp.where(inside, 1.0, member)
        size = jnp.where(doc == i, counts[i].astype(jnp.float32), size)
        begin = stop
    column = lax.broadcasted_iota(jnp.int32, (LANES, LANES), 0)
    query = lax.broadcasted_iota(jnp.int32, (LANES, LANES), 1)
    same = ((column >= query * RANK) & (column < (query + 1) * RANK)).astype(jnp.float32)

    send(to_y.at[f], from_y.at[f], end_s.at[0], end_r.at[0], dev(pp=1 - p)).wait_recv()
    send(to_y.at[f], from_y.at[1 - f], end_s.at[1], end_r.at[1], dev(pp=1 - p)).wait_recv()
    ends[2].wait_recv()
    total = (
        proj[:, p, :, half(f)] + from_sib[...]
        + from_y[0].astype(jnp.float32) + from_y[1].astype(jnp.float32)
    )
    exact = dict(precision=lax.Precision.HIGHEST, preferred_element_type=jnp.float32)
    sums = jnp.dot(jnp.dot(member, total[0] * total[1], **exact), same, **exact)
    sums = sums / jnp.sqrt(RANK * size)
    out[...] = sums[:out.shape[0], :out.shape[1]]

    gather_sent(block1, line1_s, line1_r, x1_s, x1_r)
    gather_sent(block2, line2_s, line2_r, x2_s, x2_r)

    def twins(db, carry):
        twin(db // nx, db % nx, f).wait_send()
        return carry

    lax.fori_loop(0, nd, twins, 0)

    def swaps(db, carry):
        swap_a(db, p).wait_send()
        swap_g(db, p).wait_send()
        return carry

    lax.fori_loop(0, nd, swaps, 0)
    for copy in ends:
        copy.wait_send()


def with_kernel(nz, nx, acts, grads, lengths, basis_a, basis_g, coef_a, coef_g, eig_a, eig_g):
    stack = jnp.concatenate([scaled(coef_a, eig_a), scaled(coef_g, eig_g)], axis=0)
    rows_a, rows_g = basis_a.shape[1], basis_g.shape[1]
    tok_rows, docs = acts.shape[0], lengths.shape[1]
    nd = nz * nx
    half_a, half_g = rows_a // 2, rows_g // 2
    wide = -(-half_a // LANES) * LANES
    owned = coef_a.shape[1] // 2 // RANK
    bf, f32, dma = jnp.bfloat16, jnp.float32, pltpu.SemaphoreType.DMA
    vmem = pltpu.VMEM
    anywhere = pl.BlockSpec(memory_space=pl.ANY)
    return pl.pallas_call(
        functools.partial(kernel, (nz, nx, rows_a, rows_g, docs)),
        out_shape=jax.ShapeDtypeStruct((docs, owned), f32),
        in_specs=[
            pl.BlockSpec(memory_space=pltpu.SMEM), pl.BlockSpec(memory_space=vmem),
            anywhere, anywhere, anywhere, anywhere,
        ],
        out_specs=pl.BlockSpec(memory_space=vmem),
        scratch_shapes=[
            vmem((nz, nx, 2, rows_a + rows_g, LANES), bf),
            vmem((nz, rows_a, nx * 2 * rows_a), bf),
            vmem(basis_g.shape[1:], bf),
            vmem((rows_a, LANES), f32),
            vmem((rows_g, LANES), f32),
            vmem((half_a + half_g, LANES), bf),
            vmem((nz, nx, 2, half_a + half_g, LANES), bf),
            vmem((wide, 2 * LANES), bf),
            vmem((2, nd, tok_rows, wide), bf),
            vmem((2, nd, tok_rows, half_g), bf),
            vmem((2, 2, tok_rows, 2 * LANES), f32),
            vmem((2, tok_rows, LANES), f32),
            vmem((2, 2, tok_rows, LANES), bf),
            vmem((2, 2, tok_rows, LANES), bf),
            dma((nz,)), dma, dma,
            dma((2, nz + 1)), dma((2, nz + 1)), dma((nz,)), dma((nz,)), dma((nz, nx)), dma((nz, nx)),
            dma((2, nz + 1)), dma((2, nz + 1)), dma((nz,)), dma((nz,)), dma, dma,
            dma((nd,)), dma((nd,)), dma((nd,)), dma((nd,)), dma((nd,)), dma((nd,)),
            dma((3,)), dma((3,)),
        ],
        compiler_params=pltpu.CompilerParams(
            collective_id=0, has_side_effects=True, vmem_limit_bytes=56 * 2**20
        ),
        cost_estimate=pl.CostEstimate(
            flops=2 * rows_a * basis_a.shape[2] * LANES, transcendentals=0,
            bytes_accessed=2 * basis_a.size,
        ),
    )(lengths, stack, acts, grads, basis_a, basis_g)


def chosen(sizes, *arrays):
    acts, grads, lengths, basis_a, basis_g, coef_a = arrays[:6]
    rows_a, rows_g = basis_a.shape[1], basis_g.shape[1]
    nx = 2
    fits = (
        sizes["parts"] == 2 and sizes["fac"] == 2 and sizes["dp"] % nx == 0
        and coef_a.shape[1] == 2 * LANES
        and rows_a % LANES == 0 and rows_g % (2 * LANES) == 0 and acts.shape[0] % 16 == 0
        and coef_a.shape[0] == rows_a and lengths.shape[1] <= 8
    )
    if not fits:
        return on_device(*arrays)
    return with_kernel(sizes["dp"] // nx, nx, *arrays)


def solution(mesh):
    placed = (
        P(("parts", "dp"), "fac"),
        P(("parts", "dp"), "fac"),
        P(("parts", "dp"), None),
        P("fac", "dp", None),
        P("fac", "dp", None),
        P(("dp", "fac"), None),
        P(("dp", "fac"), None),
        P(("dp", "fac")),
        P(("dp", "fac")),
    )
    return jax.shard_map(
        functools.partial(chosen, dict(mesh.shape)),
        mesh=mesh, in_specs=placed, out_specs=P(("parts", "dp"), "fac"), check_vma=False,
    )
```

```python
import functools

import jax
import jax.numpy as jnp
from jax import lax
from jax.experimental import pallas as pl
from jax.experimental.pallas import tpu as pltpu
from jax.sharding import PartitionSpec as P

RANK = 32
LANES = 128


damping = 0.1


def scaled(coef, eig):
    return (coef.astype(jnp.float32) / (eig[:, None] + damping)).astype(jnp.bfloat16)


def on_device(acts, grads, lengths, basis_a, basis_g, coef_a, coef_g, eig_a, eig_g):
    scaled_a = scaled(coef_a, eig_a)
    scaled_g = scaled(coef_g, eig_g)
    part_a = lax.all_gather(scaled_a, ("dp", "fac"), axis=0, tiled=True)
    part_g = lax.all_gather(scaled_g, ("dp", "fac"), axis=0, tiled=True)
    factor_a = jnp.dot(basis_a[0], part_a, preferred_element_type=jnp.float32).astype(jnp.bfloat16)
    factor_g = jnp.dot(basis_g[0], part_g, preferred_element_type=jnp.float32).astype(jnp.bfloat16)
    proj_a = jnp.dot(
        acts,
        lax.all_gather(factor_a, "dp", axis=0, tiled=True),
        preferred_element_type=jnp.float32,
    )
    proj_g = jnp.dot(
        grads,
        lax.all_gather(factor_g, "dp", axis=0, tiled=True),
        preferred_element_type=jnp.float32,
    )
    share_a = lax.psum_scatter(proj_a, "fac", scatter_dimension=1, tiled=True)
    share_g = lax.psum_scatter(proj_g, "fac", scatter_dimension=1, tiled=True)
    tok_rows = acts.shape[0]
    owned_queries = share_a.shape[1] // RANK
    products = (share_a * share_g).reshape(tok_rows, owned_queries, RANK).sum(axis=2)
    counts = lengths[0]
    docs = counts.shape[0]
    before = jnp.arange(docs)[:, None] <= jnp.arange(docs)[None, :]
    doc_ends = jnp.sum(jnp.where(before, counts[:, None], 0), axis=0)
    doc_starts = doc_ends - counts
    position = jnp.arange(tok_rows, dtype=jnp.int32)
    member = (
        (position[:, None] >= doc_starts[None, :]) & (position[:, None] < doc_ends[None, :])
    ).astype(jnp.float32)
    sums = jnp.einsum("td,tq->dq", member, products, precision=lax.Precision.HIGHEST)
    divisor = jnp.sqrt(RANK * counts.astype(jnp.float32))
    return sums / divisor[:, None]


def kernel(
    dims, len_ref, coef_a, coef_g, eig_a, eig_g, acts, grads, basis_a, basis_g, out,
    coefs, panel_a, panel_g, sum_a, sum_g, give, facs, padded, toks_a, toks_g,
    proj, from_sib, to_y, from_y,
    pa_sem, pg_sem,
    line1_s, line1_r, x1_s, x1_r, sib_s, sib_r,
    line2_s, line2_r, x2_s, x2_r, y_s, y_r,
    ta_l, ta_s, ta_r, tg_l, tg_s, tg_r, end_s, end_r,
):
    nz, nx, rows_a, rows_g, docs = dims
    p, d, f = lax.axis_index("parts"), lax.axis_index("dp"), lax.axis_index("fac")
    z, x = d // nx, d % nx
    nd = nz * nx
    half_a, half_g = rows_a // 2, rows_g // 2
    wide = toks_a.shape[3]
    tok_rows = acts.shape[0]

    def dev(pp=None, zz=None, xx=None, ff=None):
        zz = z if zz is None else zz
        xx = x if xx is None else xx
        return (p if pp is None else pp, zz * nx + xx, f if ff is None else ff)

    def send(src, dst, s, r, where):
        return pltpu.make_async_remote_copy(
            src_ref=src, dst_ref=dst, send_sem=s, recv_sem=r,
            device_id=where, device_id_type=pl.DeviceIdType.MESH,
        )

    deep = nx * 2 * rows_a

    def load_panel(zb):
        return pltpu.make_async_copy(
            basis_a.at[0, :, pl.ds(pl.multiple_of(zb * deep, LANES), deep)],
            panel_a.at[zb], pa_sem.at[zb],
        )

    load_g = pltpu.make_async_copy(basis_g.at[0], panel_g, pg_sem)
    load_g.start()
    for s in range(nz):
        load_panel(lax.rem(z + s, nz)).start()

    def scale(coef, eig, first):
        for at in range(0, coef.shape[0], LANES):
            divisor = jnp.broadcast_to(eig[pl.ds(at, LANES)][None, :] + damping, (LANES, LANES)).T
            rows = coef[at:at + LANES, pl.ds(pl.multiple_of(p * LANES, LANES), LANES)]
            coefs[z, x, f, first + at:first + at + LANES] = (
                rows.astype(jnp.float32) / divisor
            ).astype(jnp.bfloat16)

    barrier = pltpu.get_barrier_semaphore()
    for where in (dev(pp=1 - p), dev(pp=1 - p, ff=1 - f), dev(ff=1 - f), dev(xx=1 - x)):
        pl.semaphore_signal(barrier, inc=1, device_id=where, device_id_type=pl.DeviceIdType.MESH)

    @pl.when(z > 0)
    def _():
        pl.semaphore_signal(
            barrier, inc=1, device_id=dev(zz=z - 1), device_id_type=pl.DeviceIdType.MESH
        )

    @pl.when(z < nz - 1)
    def _():
        pl.semaphore_signal(
            barrier, inc=1, device_id=dev(zz=z + 1), device_id_type=pl.DeviceIdType.MESH
        )

    scale(coef_a, eig_a, 0)
    scale(coef_g, eig_g, rows_a)
    pl.semaphore_wait(barrier, 4 + jnp.where(z > 0, 1, 0) + jnp.where(z < nz - 1, 1, 0))

    def line(block, ss, rr, up, step, h):
        zb = z - (step - 1) if up else z + (step - 1)
        k = 0 if up else 1
        return send(block(zb, x, h), block(zb, x, h), ss.at[k, step, h], rr.at[k, step, h],
                    dev(zz=z + 1 if up else z - 1))

    def landed(block, ss, rr, up, step, h):
        zb = z - step if up else z + step
        k = 0 if up else 1
        return send(block(zb, x, h), block(zb, x, h), ss.at[k, step, h], rr.at[k, step, h],
                    dev(zz=z - 1 if up else z + 1))

    def across(block, ss, rr, zb, xb, h):
        return send(block(zb, xb, h), block(zb, xb, h), ss.at[zb, h], rr.at[zb, h],
                    dev(xx=1 - x))

    def block1(zb, xb, h, ff=None):
        chunk = (rows_a + rows_g) // 2
        return coefs.at[zb, xb, f if ff is None else ff, pl.ds(h * chunk, chunk)]

    def twin(zb, xb, ff, h):
        return send(block1(zb, xb, h, ff), block1(zb, xb, h, ff),
                    sib_s.at[zb, xb, h], sib_r.at[zb, xb, h], dev(ff=1 - f))

    def gather(block, ls, lr, xs, xr, extra, use, between):
        def pass_on(zb, h):
            across(block, xs, xr, zb, x, h).start()
            extra(zb, x, h)

        def begin(h):
            @pl.when(z < nz - 1)
            def _():
                line(block, ls, lr, True, 1, h).start()

            @pl.when(z > 0)
            def _():
                line(block, ls, lr, False, 1, h).start()

            pass_on(z, h)

        begin(0)
        between()
        begin(1)

        def step(s, carry):
            for h in range(2):
                @pl.when((s < nz) & (z - s >= 0))
                def _():
                    landed(block, ls, lr, True, s, h).wait_recv()

                    @pl.when(z < nz - 1)
                    def _():
                        line(block, ls, lr, True, s + 1, h).start()

                    pass_on(z - s, h)

                @pl.when((s < nz) & (z + s < nz))
                def _():
                    landed(block, ls, lr, False, s, h).wait_recv()

                    @pl.when(z > 0)
                    def _():
                        line(block, ls, lr, False, s + 1, h).start()

                    pass_on(z + s, h)

            def side(j, c):
                zb = z + (s - 1) * (2 * j - 1)

                @pl.when((zb >= 0) & (zb < nz) & ((s > 1) | (j == 0)))
                def _():
                    for h in range(2):
                        across(block, xs, xr, zb, 1 - x, h).wait_recv()
                        extra(zb, 1 - x, h)
                    use(zb)

                return c

            return lax.fori_loop(0, 2, side, carry)

        lax.fori_loop(1, nz + 1, step, 0)

    def gather_sent(block, ls, lr, xs, xr):
        def step(s, carry):
            for h in range(2):
                @pl.when((z < nz - 1) & (z - s + 1 >= 0))
                def _():
                    line(block, ls, lr, True, s, h).wait_send()

                @pl.when((z > 0) & (z + s - 1 < nz))
                def _():
                    line(block, ls, lr, False, s, h).wait_send()

            return carry

        lax.fori_loop(1, nz, step, 0)

        def crossing(zb, carry):
            for h in range(2):
                across(block, xs, xr, zb, x, h).wait_send()
            return carry

        lax.fori_loop(0, nz, crossing, 0)

    step_a = rows_a - wide

    def cols_a(db, q):
        return pl.ds(pl.multiple_of(db * rows_a + q * step_a, LANES), wide)

    def cols_g(db, q):
        return pl.ds(pl.multiple_of(db * rows_g + q * half_g, LANES), half_g)

    def own_a(db):
        return pltpu.make_async_copy(acts.at[:, cols_a(db, p)], toks_a.at[p, db], ta_l.at[db])

    def own_g(db):
        return pltpu.make_async_copy(grads.at[:, cols_g(db, p)], toks_g.at[p, db], tg_l.at[db])

    def swap_a(db, q):
        return send(acts.at[:, cols_a(db, 1 - p)], toks_a.at[q, db], ta_s.at[db], ta_r.at[db],
                    dev(pp=1 - p))

    def swap_g(db, q):
        return send(grads.at[:, cols_g(db, 1 - p)], toks_g.at[q, db], tg_s.at[db], tg_r.at[db],
                    dev(pp=1 - p))

    early = nd - nx

    def start_swaps(lo, hi):
        def body(i, carry):
            near = jnp.where(2 * z < nz, z + i // nx, z + nz - i // nx)
            db = lax.rem(near, nz) * nx + i % nx
            swap_a(db, p).start()
            swap_g(db, p).start()
            return carry

        lax.fori_loop(lo, hi, body, 0)

    def extra1(zb, xb, h):
        twin(zb, xb, f, h).start()

    sum_a[...] = jnp.zeros_like(sum_a)
    sum_g[...] = jnp.zeros_like(sum_g)
    padded[...] = jnp.zeros_like(padded)
    proj[...] = jnp.zeros_like(proj)

    def use1(zb):
        load_panel(zb).wait()

        @pl.when(zb == z)
        def _():
            load_g.wait()

        for xb in range(nx):
            for h in range(2):
                twin(zb, xb, 1 - f, h).wait_recv()
        total_a, total_g = sum_a[...], sum_g[...]
        for i in range(nx * 2):
            block = coefs.at[zb, i // 2, i % 2]
            total_a += jnp.dot(
                panel_a[zb, :, i * rows_a:(i + 1) * rows_a], block[:rows_a],
                preferred_element_type=jnp.float32,
            )
            at = pl.multiple_of((zb * nx * 2 + i) * rows_g, LANES)
            total_g += jnp.dot(
                panel_g[:, pl.ds(at, rows_g)], block[rows_a:],
                preferred_element_type=jnp.float32,
            )
        sum_a[...] = total_a
        sum_g[...] = total_g

    start_swaps(0, early)

    def start_own(db, carry):
        own_a(db).start()
        own_g(db).start()
        return carry

    lax.fori_loop(0, nd, start_own, 0)
    gather(block1, line1_s, line1_r, x1_s, x1_r, extra1, use1, lambda: None)

    def halves(q):
        return (
            sum_a[pl.ds(pl.multiple_of(q * half_a, 16), half_a), :].astype(jnp.bfloat16),
            sum_g[pl.ds(pl.multiple_of(q * half_g, 16), half_g), :].astype(jnp.bfloat16),
        )

    give_a, give_g = halves(1 - p)
    give[:half_a] = give_a
    give[half_a:] = give_g
    send(give, facs.at[z, x, p], y_s, y_r, dev(pp=1 - p)).start()
    keep_a, keep_g = halves(p)
    facs[z, x, p, :half_a] = keep_a
    facs[z, x, p, half_a:] = keep_g
    start_swaps(early, nd)

    def block2(zb, xb, h):
        return facs.at[zb, xb, p if h == 0 else 1 - p]

    def between2():
        send(give, facs.at[z, x, 1 - p], y_s, y_r, dev(pp=1 - p)).wait_recv()

    lead = half_a - step_a

    def use2(zb):
        for xb in range(nx):
            db = zb * nx + xb
            own_a(db).wait()
            own_g(db).wait()
            swap_a(db, 1 - p).wait_recv()
            swap_g(db, 1 - p).wait_recv()
            rows = pl.ds(pl.multiple_of(p * lead, 16), half_a)
            for c in range(2):
                padded[rows, c * LANES:(c + 1) * LANES] = facs[zb, xb, c, :half_a]
            fac_g = jnp.concatenate([facs[zb, xb, c, half_a:] for c in range(2)], axis=1)
            fac_a = padded[...]
            for q in range(2):
                proj[0, q] += jnp.dot(toks_a[q, db], fac_a, preferred_element_type=jnp.float32)
                proj[1, q] += jnp.dot(toks_g[q, db], fac_g, preferred_element_type=jnp.float32)

    gather(block2, line2_s, line2_r, x2_s, x2_r, lambda zb, xb, h: None, use2, between2)

    def half(q):
        return pl.ds(pl.multiple_of(q * LANES, LANES), LANES)

    for ff in range(2):
        to_y[ff] = proj[:, 1 - p, :, ff * LANES:(ff + 1) * LANES].astype(jnp.bfloat16)
    ends = [
        send(to_y.at[f], from_y.at[f], end_s.at[0], end_r.at[0], dev(pp=1 - p)),
        send(to_y.at[1 - f], from_y.at[f], end_s.at[1], end_r.at[1], dev(pp=1 - p, ff=1 - f)),
        send(proj.at[:, p, :, half(1 - f)], from_sib, end_s.at[2], end_r.at[2], dev(ff=1 - f)),
    ]
    for copy in ends:
        copy.start()

    counts = [len_ref[0, i] for i in range(docs)]
    row = lax.broadcasted_iota(jnp.int32, (8, tok_rows), 0)
    position = lax.broadcasted_iota(jnp.int32, (8, tok_rows), 1)
    doc = lax.broadcasted_iota(jnp.int32, (8, LANES), 0)
    member = jnp.zeros((8, tok_rows), jnp.float32)
    size = jnp.ones((8, LANES), jnp.float32)
    begin = jnp.int32(0)
    for i in range(docs):
        stop = begin + counts[i]
        inside = (row == i) & (position >= begin) & (position < stop)
        member = jnp.where(inside, 1.0, member)
        size = jnp.where(doc == i, counts[i].astype(jnp.float32), size)
        begin = stop
    column = lax.broadcasted_iota(jnp.int32, (LANES, LANES), 0)
    query = lax.broadcasted_iota(jnp.int32, (LANES, LANES), 1)
    same = ((column >= query * RANK) & (column < (query + 1) * RANK)).astype(jnp.float32)

    send(to_y.at[f], from_y.at[f], end_s.at[0], end_r.at[0], dev(pp=1 - p)).wait_recv()
    send(to_y.at[f], from_y.at[1 - f], end_s.at[1], end_r.at[1], dev(pp=1 - p)).wait_recv()
    ends[2].wait_recv()
    total = (
        proj[:, p, :, half(f)] + from_sib[...]
        + from_y[0].astype(jnp.float32) + from_y[1].astype(jnp.float32)
    )
    exact = dict(precision=lax.Precision.HIGHEST, preferred_element_type=jnp.float32)
    sums = jnp.dot(jnp.dot(member, total[0] * total[1], **exact), same, **exact)
    sums = sums / jnp.sqrt(RANK * size)
    out[...] = sums[:out.shape[0], :out.shape[1]]

    gather_sent(block1, line1_s, line1_r, x1_s, x1_r)
    gather_sent(block2, line2_s, line2_r, x2_s, x2_r)

    def twins(db, carry):
        for h in range(2):
            twin(db // nx, db % nx, f, h).wait_send()
        return carry

    lax.fori_loop(0, nd, twins, 0)

    def swaps(db, carry):
        swap_a(db, p).wait_send()
        swap_g(db, p).wait_send()
        return carry

    lax.fori_loop(0, nd, swaps, 0)
    send(give, facs.at[z, x, p], y_s, y_r, dev(pp=1 - p)).wait_send()
    for copy in ends:
        copy.wait_send()


def with_kernel(nz, nx, acts, grads, lengths, basis_a, basis_g, coef_a, coef_g, eig_a, eig_g):
    rows_a, rows_g = basis_a.shape[1], basis_g.shape[1]
    tok_rows, docs = acts.shape[0], lengths.shape[1]
    nd = nz * nx
    half_a, half_g = rows_a // 2, rows_g // 2
    wide = -(-half_a // LANES) * LANES
    owned = coef_a.shape[1] // 2 // RANK
    bf, f32, dma = jnp.bfloat16, jnp.float32, pltpu.SemaphoreType.DMA
    vmem = pltpu.VMEM
    anywhere = pl.BlockSpec(memory_space=pl.ANY)
    return pl.pallas_call(
        functools.partial(kernel, (nz, nx, rows_a, rows_g, docs)),
        out_shape=jax.ShapeDtypeStruct((docs, owned), f32),
        in_specs=[
            pl.BlockSpec(memory_space=pltpu.SMEM), *[pl.BlockSpec(memory_space=vmem)] * 4,
            anywhere, anywhere, anywhere, anywhere,
        ],
        out_specs=pl.BlockSpec(memory_space=vmem),
        scratch_shapes=[
            vmem((nz, nx, 2, rows_a + rows_g, LANES), bf),
            vmem((nz, rows_a, nx * 2 * rows_a), bf),
            vmem(basis_g.shape[1:], bf),
            vmem((rows_a, LANES), f32),
            vmem((rows_g, LANES), f32),
            vmem((half_a + half_g, LANES), bf),
            vmem((nz, nx, 2, half_a + half_g, LANES), bf),
            vmem((wide, 2 * LANES), bf),
            vmem((2, nd, tok_rows, wide), bf),
            vmem((2, nd, tok_rows, half_g), bf),
            vmem((2, 2, tok_rows, 2 * LANES), f32),
            vmem((2, tok_rows, LANES), f32),
            vmem((2, 2, tok_rows, LANES), bf),
            vmem((2, 2, tok_rows, LANES), bf),
            dma((nz,)), dma,
            dma((2, nz + 1, 2)), dma((2, nz + 1, 2)), dma((nz, 2)), dma((nz, 2)),
            dma((nz, nx, 2)), dma((nz, nx, 2)),
            dma((2, nz + 1, 2)), dma((2, nz + 1, 2)), dma((nz, 2)), dma((nz, 2)), dma, dma,
            dma((nd,)), dma((nd,)), dma((nd,)), dma((nd,)), dma((nd,)), dma((nd,)),
            dma((3,)), dma((3,)),
        ],
        compiler_params=pltpu.CompilerParams(
            collective_id=0, has_side_effects=True, vmem_limit_bytes=56 * 2**20
        ),
        cost_estimate=pl.CostEstimate(
            flops=2 * rows_a * basis_a.shape[2] * LANES, transcendentals=0,
            bytes_accessed=2 * basis_a.size,
        ),
    )(lengths, coef_a, coef_g, eig_a, eig_g, acts, grads, basis_a, basis_g)


def chosen(sizes, *arrays):
    acts, grads, lengths, basis_a, basis_g, coef_a = arrays[:6]
    rows_a, rows_g = basis_a.shape[1], basis_g.shape[1]
    nx = 2
    fits = (
        sizes["parts"] == 2 and sizes["fac"] == 2 and sizes["dp"] % nx == 0
        and coef_a.shape[1] == 2 * LANES
        and rows_a % LANES == 0 and rows_g % (2 * LANES) == 0 and acts.shape[0] % 16 == 0
        and coef_a.shape[0] == rows_a and lengths.shape[1] <= 8
    )
    if not fits:
        return on_device(*arrays)
    return with_kernel(sizes["dp"] // nx, nx, *arrays)


def solution(mesh):
    placed = (
        P(("parts", "dp"), "fac"),
        P(("parts", "dp"), "fac"),
        P(("parts", "dp"), None),
        P("fac", "dp", None),
        P("fac", "dp", None),
        P(("dp", "fac"), None),
        P(("dp", "fac"), None),
        P(("dp", "fac")),
        P(("dp", "fac")),
    )
    return jax.shard_map(
        functools.partial(chosen, dict(mesh.shape)),
        mesh=mesh, in_specs=placed, out_specs=P(("parts", "dp"), "fac"), check_vma=False,
    )
```
